256 devices in a mesh: dp: 16 (over z_hi, y), mp: 16 (over x, z_lo, core).
Axes of the slice: x: 4, y: 4, z: 8 (z_hi: 4, z_lo: 2; z = z_hi * 2 + z_lo), core: 2. Of those that a mesh axis runs over, the one named last changes fastest.
Arguments:
- tokens: bfloat16 [2048, 8192], P('dp', 'mp'), may hold values from -6 to 6
- expand_weight: bfloat16 [32, 256, 1024], P('mp'), may hold values from -0.375 to 0.375
- section_weight: bfloat16 [4, 128, 2, 256, 256], P(None, 'mp'), may hold values from -0.25 to 0.25
- contract_weight: bfloat16 [32, 1024, 256], P('mp'), may hold values from -0.1875 to 0.1875
- pattern: int32 [4, 8], replicated, may hold values from 0 to 7, each once within a row
- cotangent: bfloat16 [2048, 8192], P('dp', 'mp'), may hold values from -6 to 6
Outputs:
- output: bfloat16 [2048, 8192], P('dp', 'mp')
- input_grad: bfloat16 [2048, 8192], P('dp', 'mp')
- expand_grad: bfloat16 [32, 256, 1024], P('mp', 'dp')
- section_grad: bfloat16 [4, 128, 2, 256, 256], P(None, 'mp', None, 'dp')
- contract_grad: bfloat16 [32, 1024, 256], P('mp', 'dp')
The draws below stay inside these ranges and needn't reach their ends.
Inputs may be any that keep to these rules, and one draw needn't show every extreme that they name: Each row of pattern is a permutation of 0 .. 7.
All inputs are finite; a program needn't handle non-finite values.
Results may differ from the reference program's by a relative error of at most 0.025.
Values may be sent and summed in bfloat16 or wider, within the bound.
A program may use at most 128 MiB of HBM per device.

```python
import math
import jax
import jax.numpy as jnp
from jax import lax

BLK = 256
EXPAND = 4
TOK_DEV = 128
HB_DEV = 8
SECTIONS = 4
IB = 32
NB = 128
D = 8192
TOKENS = 2048
N_DP = 16


def level_of(stream_key, dims, cuts, low, largest):
    def one(axis_at, shards_of):
        draws = jax.random.uniform(jax.random.fold_in(jax.random.fold_in(stream_key, 6), axis_at), (shards_of,), jnp.float32, low / len(cuts), largest / len(cuts))
        return jnp.repeat(jnp.exp(draws), dims[axis_at] // shards_of).reshape((-1,) + (1,) * (len(dims) - axis_at - 1))

    level = one(*cuts[0])
    for cut in cuts[1:]:
        level = level * one(*cut)
    return level


def normal_values(own_key, extent, width, bound, split=(), kind=jnp.bfloat16):
    level = level_of(own_key, extent, split, -0.22, 0.18) if split else 1.0
    drawn = jax.random.normal(own_key, extent, jnp.float32) * width * level
    return jnp.minimum(jnp.maximum(drawn, -bound), bound).astype(kind)


def setup_inputs(seed: int = 0) -> dict:
    key_of = jax.random.split(jax.random.key(seed), 7)
    tokens = normal_values(key_of[0], (TOKENS, D), 1.0, 6.0, ((0, 16), (1, 16)))
    expand_weight = normal_values(key_of[1], (IB, BLK, EXPAND * BLK), BLK ** -0.5, 0.375, ((0, 16),))
    section_weight = normal_values(key_of[2], (SECTIONS, NB, 2, BLK, BLK), (2 * BLK) ** -0.5, 0.25, ((1, 16),))
    contract_weight = normal_values(key_of[3], (IB, EXPAND * BLK, BLK), (EXPAND * BLK) ** -0.5, 0.1875, ((0, 16),))
    pattern = jax.vmap(lambda own: jax.random.permutation(own, HB_DEV))(jax.random.split(key_of[4], SECTIONS)).reshape((SECTIONS, HB_DEV)).astype(jnp.int32)
    cotangent = normal_values(key_of[5], (TOKENS, D), 1.0, 6.0, ((0, 16), (1, 16)))
    return dict(tokens=tokens, expand_weight=expand_weight, section_weight=section_weight, contract_weight=contract_weight, pattern=pattern, cotangent=cotangent)


def gelu_exact(values):
    return jax.nn.gelu(values, approximate=False)

def group_pass(tok_rows_in, cot_rows_in, expand_weight, section_weight, contract_weight, pattern):
    row_count = tok_rows_in.shape[0]
    tok_blocks = tok_rows_in.reshape(row_count, IB, BLK).astype(jnp.float32)
    expand_full = expand_weight.astype(jnp.float32)
    hidden = jnp.einsum('rmi,mio->rmo', tok_blocks, expand_full).reshape(row_count, NB, BLK).astype(jnp.bfloat16)
    block_ids = jnp.arange(NB, dtype=jnp.int32)
    owner_dev = block_ids // HB_DEV
    within = block_ids % HB_DEV
    saved = []
    mixed = None
    for section in range(SECTIONS):
        stride = HB_DEV * 2 ** section
        source = (owner_dev * HB_DEV + pattern[section][within]).astype(jnp.int32)
        paired = jnp.stack([hidden[:, source], hidden[:, jnp.bitwise_xor(source, stride)]], axis=2)
        saved.append(paired)
        mixed = jnp.einsum('rbsc,bscd->rbd', paired.astype(jnp.float32), section_weight[section].astype(jnp.float32))
        if section + 1 < SECTIONS:
            hidden = mixed.astype(jnp.bfloat16)
    activated, gelu_back = jax.vjp(gelu_exact, mixed)
    activated = activated.astype(jnp.bfloat16)
    gelu_blocks = activated.reshape(row_count, IB, EXPAND * BLK).astype(jnp.float32)
    contract_full = contract_weight.astype(jnp.float32)
    output = jnp.einsum('rje,jed->rjd', gelu_blocks, contract_full).reshape(row_count, D).astype(jnp.bfloat16)
    cot_blocks = cot_rows_in.reshape(row_count, IB, BLK).astype(jnp.float32)
    contract_term = jnp.einsum('rje,rjd->jed', gelu_blocks, cot_blocks)
    gelu_grad = jnp.einsum('rjd,jed->rje', cot_blocks, contract_full).reshape(row_count, NB, BLK)
    upstream = gelu_back(gelu_grad)[0].astype(jnp.bfloat16)
    section_terms = [None] * SECTIONS
    for section in reversed(range(SECTIONS)):
        stride = HB_DEV * 2 ** section
        up_full = upstream.astype(jnp.float32)
        section_terms[section] = jnp.einsum('rbsc,rbd->bscd', saved[section].astype(jnp.float32), up_full)
        local_part = jnp.einsum('rbd,bcd->rbc', up_full, section_weight[section, :, 0].astype(jnp.float32))
        far_part = jnp.einsum('rbd,bcd->rbc', up_full, section_weight[section, :, 1].astype(jnp.float32)).astype(jnp.bfloat16)
        inverse = jnp.argsort(pattern[section]).astype(jnp.int32)
        target = (owner_dev * HB_DEV + inverse[within]).astype(jnp.int32)
        upstream = (local_part[:, target] + far_part[:, jnp.bitwise_xor(target, stride)].astype(jnp.float32)).astype(jnp.bfloat16)
    first_grad = upstream.reshape(row_count, IB, EXPAND * BLK).astype(jnp.float32)
    expand_term = jnp.einsum('rmi,rmo->mio', tok_blocks, first_grad)
    input_grad = jnp.einsum('rmo,mio->rmi', first_grad, expand_full).reshape(row_count, D).astype(jnp.bfloat16)
    return (output, input_grad, jnp.stack(section_terms), expand_term, contract_term)

def reference(tokens, expand_weight, section_weight, contract_weight, pattern, cotangent):
    outputs = []
    input_grads = []
    totals = []
    for group_idx in range(N_DP):
        row_start = group_idx * TOK_DEV
        result = group_pass(tokens[row_start:row_start + TOK_DEV], cotangent[row_start:row_start + TOK_DEV], expand_weight, section_weight, contract_weight, pattern)
        outputs.append(result[0])
        input_grads.append(result[1])
        rounded = [lax.optimization_barrier(partial_term.astype(jnp.bfloat16)).astype(jnp.float32) for partial_term in result[2:]]
        if group_idx == 0:
            totals = rounded
        else:
            totals = [summed + extra for summed, extra in zip(totals, rounded)]
    grad_scale = 1.0 / math.sqrt(TOKENS)
    return (jnp.concatenate(outputs, axis=0), jnp.concatenate(input_grads, axis=0), (totals[1] * grad_scale).astype(jnp.bfloat16), (totals[0] * grad_scale).astype(jnp.bfloat16), (totals[2] * grad_scale).astype(jnp.bfloat16))
```

```python
import math

import jax
import jax.numpy as jnp
from jax import lax
from jax.experimental import pallas as pl
from jax.experimental.pallas import tpu as pltpu
from jax.sharding import PartitionSpec as P

MESH = pl.DeviceIdType.MESH
BF16, F32 = jnp.bfloat16, jnp.float32
BLK = 256
ROWS = 128
CHUNKS = 2
PIECE = ROWS // CHUNKS
SECTIONS = 4
HIDDEN = 8
HALF = 4
SHARDS = 16
COPIES = 96


def dot(left, right, left_dim, right_dim):
    return lax.dot_general(
        left, right, (((left_dim,), (right_dim,)), ((), ())), preferred_element_type=F32
    )


def each(count, unroll, step):
    def several(at, carry):
        for more in range(unroll):
            step(at * unroll + more)
        return carry

    lax.fori_loop(0, count // unroll, several, 0)


def kernel(
    scale, pattern, tokens_hbm, expand_hbm, section_hbm, contract_hbm, cot_hbm,
    out_hbm, in_grad_hbm, expand_grad_hbm, section_grad_hbm, contract_grad_hbm,
    tok, cot, expand_w, section_w, contract_w, chosen, paired, grads, act, hidden, total, gelu_grad,
    u_out, u_in, part_s, part_c, part_e, r1_s, r1_c, r1_e, r2_s, r2_c, r2_e, r3_s, r3_c, r3_e,
    fin_s, fin_c, fin_e, far_s, far_c, far_e, out_v, in_grad_v,
    send_sem, recv_sem, local_sem,
):
    dp, mp = lax.axis_index("dp"), lax.axis_index("mp")
    core = mp % 2
    zh, y = dp // 4, dp % 4
    near_y, cross_y = y + 1 - 2 * (y % 2), 3 - y
    near_z, cross_z = zh + 1 - 2 * (zh % 2), 3 - zh
    ya = near_y + core * (cross_y - near_y)
    yb = cross_y + core * (near_y - cross_y)
    za = near_z + core * (cross_z - near_z)
    zb = cross_z + core * (near_z - cross_z)
    to_ya, to_yb = (zh * 4 + ya, mp), (zh * 4 + yb, mp)
    to_za, to_zb = (za * 4 + y, mp), (zb * 4 + y, mp)
    across = [
        (dp, mp + 2**k - 2 * 2**k * ((mp // 2**k) % 2)) for k in range(SECTIONS)
    ]
    half = (y + y // 2) % 2 * (1 - core) + y // 2 * core
    mine, theirs = half * HALF, (1 - half) * HALF

    def split(own, other):
        low, high = (own + other) % 2, (own // 2 + other // 2) % 2
        both = (low + high) % 2
        return both + core * (high - both), high + core * (both - high)

    slot = []
    for shard in range(SHARDS):
        z_first, z_second = split(zh, shard // 4)
        y_last, y_first = split(y, shard % 4)
        slot.append(8 * y_first + 4 * z_first + 2 * z_second + y_last)

    loads, sends = [], []

    def load(src, dst):
        copy = pltpu.make_async_copy(src, dst, local_sem.at[len(loads)])
        copy.start()
        loads.append(copy)
        return copy

    def send(src, dst, device):
        at = len(sends)
        copy = pltpu.make_async_remote_copy(
            src_ref=src,
            dst_ref=dst,
            send_sem=send_sem.at[at],
            recv_sem=recv_sem.at[at],
            device_id=device,
            device_id_type=MESH,
        )
        copy.start()
        sends.append(copy)
        return copy

    tok_in = [load(tokens_hbm.at[:, pl.ds(j * BLK, BLK)], tok.at[j, pl.ds(0, ROWS)]) for j in range(2)]
    expand_in = load(expand_hbm, expand_w)
    section_in = [load(section_hbm.at[0], section_w.at[0])]
    cot_in = [load(cot_hbm.at[:, pl.ds(j * BLK, BLK)], cot.at[j, pl.ds(0, ROWS)]) for j in range(2)]
    contract_in = load(contract_hbm, contract_w)
    section_in += [load(section_hbm.at[k], section_w.at[k]) for k in range(1, SECTIONS)]

    barrier = pltpu.get_barrier_semaphore()
    peers = [*across, to_ya, to_yb, to_za, to_zb]
    for device in peers:
        pl.semaphore_signal(barrier, inc=1, device_id=device, device_id_type=MESH)

    inverse = []
    for k in range(SECTIONS):
        row = []
        for c in range(HIDDEN):
            place = jnp.int32(0)
            for m in range(1, HIDDEN):
                place = jnp.where(pattern[k, m] == c, jnp.int32(m), place)
            row.append(place)
        inverse.append(row)

    def rows(piece):
        return pl.ds(piece * PIECE, PIECE)

    def expand(piece):
        for j in range(2):
            source = tok[j, rows(piece)]
            for i in range(4):
                hidden[j * 4 + i, rows(piece)] = dot(
                    source, expand_w[j, :, i * BLK : (i + 1) * BLK], 1, 0
                ).astype(BF16)

    def choose(k, piece):
        for m in range(HIDDEN):
            chosen[k, m, rows(piece)] = hidden[pattern[k, m], rows(piece)]

    def exchange(k, piece):
        return send(
            chosen.at[k, :, rows(piece)], paired.at[k, :, rows(piece)], across[k]
        )

    def own_part(k, piece):
        def one(b):
            total[b, rows(piece)] = dot(
                chosen[k, b, rows(piece)], section_w[k, b, 0], 1, 0
            )

        each(HIDDEN, 4, one)

    def pair_part(k, piece, use):
        def one(b):
            use(
                b,
                total[b, rows(piece)]
                + dot(paired[k, b, rows(piece)], section_w[k, b, 1], 1, 0),
            )

        each(HIDDEN, 4, one)

    def to_hidden(piece):
        def use(b, value):
            hidden[b, rows(piece)] = value.astype(BF16)

        return use

    def to_gelu(piece):
        def use(b, z):
            below = 0.5 * (1.0 + lax.erf(z * math.sqrt(0.5)))
            act[b, rows(piece)] = (z * below).astype(BF16)
            slope = below + z * (jnp.exp(-0.5 * z * z) * (1.0 / math.sqrt(2.0 * math.pi)))
            grads[SECTIONS, b, rows(piece)] = (
                gelu_grad[b, rows(piece)] * slope
            ).astype(BF16)

        return use

    def share(ref):
        part = ref.at[pl.ds(theirs, HALF)]
        return send(part.at[:, pl.ds(0, ROWS)], part.at[:, pl.ds(ROWS, ROWS)], to_ya)

    def share_feature(ref):
        part = ref.at[1 - half]
        return send(part.at[pl.ds(0, ROWS)], part.at[pl.ds(ROWS, ROWS)], to_ya)

    def back(k, piece):
        def far(b):
            u_out[k, b, rows(piece)] = dot(
                grads[k + 1, b, rows(piece)], section_w[k, b, 1], 1, 1
            ).astype(BF16)

        each(HIDDEN, 4, far)
        copy = send(u_out.at[k, :, rows(piece)], u_in.at[k, :, rows(piece)], across[k])

        def near(b):
            total[b, rows(piece)] = dot(
                grads[k + 1, b, rows(piece)], section_w[k, b, 0], 1, 1
            )

        each(HIDDEN, 4, near)
        return copy

    def gather_back(k, piece):
        def one(b):
            hidden[b, rows(piece)] = (
                total[b, rows(piece)] + u_in[k, b, rows(piece)].astype(F32)
            ).astype(BF16)

        each(HIDDEN, 4, one)
        for c in range(HIDDEN):
            grads[k, c, rows(piece)] = hidden[inverse[k][c], rows(piece)]

    class Reduction:
        def __init__(self, part, r1, r2, r3, fin, far, unroll):
            self.part, self.r1, self.r2, self.r3 = part, r1, r2, r3
            self.fin, self.far, self.unroll = fin, far, unroll

        def first(self):
            self.copy = send(self.part.at[pl.ds(8, 8)], self.r1, to_yb)

        def add(self, received, count):
            def one(at):
                self.part[at] = (
                    self.part[at].astype(F32) + received[at].astype(F32)
                ).astype(BF16)

            each(count, self.unroll, one)

        def second(self):
            self.copy.wait_recv()
            self.add(self.r1, 8)
            self.copy = send(self.part.at[pl.ds(4, 4)], self.r2, to_za)

        def third(self):
            self.copy.wait_recv()
            self.add(self.r2, 4)
            self.copy = send(self.part.at[pl.ds(2, 2)], self.r3, to_zb)

        def fourth(self, own):
            self.copy.wait_recv()
            for at in range(2):
                self.fin[at] = (
                    (self.part[at].astype(F32) + self.r3[at].astype(F32)) * scale
                ).astype(BF16)
            self.copy = send(self.fin.at[1], self.far, to_ya)
            load(self.fin.at[0], own)

        def fifth(self, other):
            self.copy.wait_recv()
            load(self.far, other)

    reduce_s = [
        Reduction(part_s.at[k], r1_s.at[k], r2_s.at[k], r3_s.at[k], fin_s.at[k], far_s.at[k], 1)
        for k in range(SECTIONS)
    ]
    reduce_c = Reduction(part_c, r1_c, r2_c, r3_c, fin_c, far_c, 2)
    reduce_e = Reduction(part_e, r1_e, r2_e, r3_e, fin_e, far_e, 2)

    def section_terms(k):
        for i in range(HALF):
            upstream = grads[k + 1, mine + i]
            for s, ref in enumerate((chosen, paired)):
                term = dot(ref[k, mine + i], upstream, 0, 0).astype(BF16)
                for shard in range(SHARDS):
                    part_s[k, slot[shard], i, s] = term[shard * 16 : (shard + 1) * 16]
        reduce_s[k].first()

    def contract_terms():
        for i in range(HALF):
            term = dot(act[mine + i], cot[half], 0, 0).astype(BF16)
            for q in range(4):
                part_c[slot[i * 4 + q]] = term[q * 64 : (q + 1) * 64]
        reduce_c.first()

    def expand_terms():
        for i in range(HALF):
            term = dot(tok[half], grads[0, mine + i], 0, 0).astype(BF16)
            for shard in range(SHARDS):
                part_e[slot[shard], :, i * BLK : (i + 1) * BLK] = term[shard * 16 : (shard + 1) * 16]
        reduce_e.first()

    pieces = range(CHUNKS)
    coming = [None] * CHUNKS
    shared = {}

    for copy in tok_in:
        copy.wait()
    expand_in.wait()
    for piece in pieces:
        expand(piece)
        choose(0, piece)
        if piece == 0:
            pl.semaphore_wait(barrier, len(peers))
        coming[piece] = exchange(0, piece)
        if piece == 0:
            section_in[0].wait()
        own_part(0, piece)
    shared["tok"] = share_feature(tok)
    shared["own", 0] = share(chosen.at[0])
    for k in range(SECTIONS - 1):
        section_in[k + 1].wait()
        for piece in pieces:
            coming[piece].wait_recv()
            pair_part(k, piece, to_hidden(piece))
            choose(k + 1, piece)
            coming[piece] = exchange(k + 1, piece)
            own_part(k + 1, piece)
        shared["pair", k] = share(paired.at[k])
        shared["own", k + 1] = share(chosen.at[k + 1])
        if k == 0:
            for copy in cot_in:
                copy.wait()
            contract_in.wait()
            shared["cot"] = share_feature(cot)

            def gelu_grads(j):
                source = cot[j, pl.ds(0, ROWS)]
                for i in range(4):
                    gelu_grad[j * 4 + i] = dot(
                        source, contract_w[j, i * BLK : (i + 1) * BLK], 1, 1
                    )

            each(2, 1, gelu_grads)

    for piece in pieces:
        coming[piece].wait_recv()
        pair_part(SECTIONS - 1, piece, to_gelu(piece))
        coming[piece] = back(SECTIONS - 1, piece)
    shared["grad", SECTIONS] = share(grads.at[SECTIONS])
    shared["act"] = share(act)
    shared["pair", SECTIONS - 1] = share(paired.at[SECTIONS - 1])

    def outputs(j):
        sums = sum(
            dot(act[j * 4 + i, pl.ds(0, ROWS)], contract_w[j, i * BLK : (i + 1) * BLK], 1, 0)
            for i in range(4)
        )
        out_v[j] = sums.astype(BF16)

    each(2, 1, outputs)
    for j in range(2):
        load(out_v.at[j], out_hbm.at[:, pl.ds(j * BLK, BLK)])

    def await_shared(*names):
        for name in names:
            shared[name].wait_recv()

    def section_first(k):
        await_shared(("grad", k + 1), ("own", k), ("pair", k))
        section_terms(k)

    def stage(k):
        for piece in pieces:
            coming[piece].wait_recv()
            gather_back(k, piece)
            if k:
                coming[piece] = back(k - 1, piece)
        shared["grad", k] = share(grads.at[k])

    def own_grad(k):
        return section_grad_hbm.at[k, pl.ds(mine, HALF)]

    def far_grad(k):
        return section_grad_hbm.at[k, pl.ds(theirs, HALF)]

    stage(3)
    await_shared("act", "cot")
    contract_terms()
    section_first(3)
    stage(2)
    reduce_c.second()
    section_first(2)
    reduce_s[3].second()
    stage(1)
    stage(0)
    reduce_c.third()
    reduce_s[3].third()
    section_first(1)
    reduce_s[2].second()
    section_first(0)
    await_shared("tok")
    await_shared(("grad", 0))
    expand_terms()
    for j in range(2):
        sums = sum(
            dot(grads[0, j * 4 + i, pl.ds(0, ROWS)], expand_w[j, :, i * BLK : (i + 1) * BLK], 1, 1)
            for i in range(4)
        )
        in_grad_v[j] = sums.astype(BF16)
        load(in_grad_v.at[j], in_grad_hbm.at[:, pl.ds(j * BLK, BLK)])
    reduce_s[2].third()
    reduce_c.fourth(contract_grad_hbm.at[half])
    reduce_s[3].fourth(own_grad(3))
    reduce_s[1].second()
    reduce_s[0].second()
    reduce_e.second()
    reduce_s[2].fourth(own_grad(2))
    reduce_s[1].third()
    reduce_s[0].third()
    reduce_e.third()
    reduce_c.fifth(contract_grad_hbm.at[1 - half])
    reduce_s[3].fifth(far_grad(3))
    reduce_s[1].fourth(own_grad(1))
    reduce_s[0].fourth(own_grad(0))
    reduce_e.fourth(expand_grad_hbm.at[half])
    reduce_s[2].fifth(far_grad(2))
    reduce_s[1].fifth(far_grad(1))
    reduce_s[0].fifth(far_grad(0))
    reduce_e.fifth(expand_grad_hbm.at[1 - half])
    for copy in sends:
        copy.wait_send()
    for copy in loads[len(tok_in) + len(cot_in) + 2 + SECTIONS :]:
        copy.wait()


def body(tokens, expand_weight, section_weight, contract_weight, pattern, cotangent):
    scale = 1.0 / math.sqrt(tokens.shape[0] * lax.axis_size("dp"))
    hbm = pl.BlockSpec(memory_space=pl.ANY)

    def vmem(*shape, dtype=BF16):
        return pltpu.VMEM(shape, dtype)

    sec, con, exp = (HALF, 2, 16, BLK), (64, BLK), (16, 4 * BLK)
    scratch = [
        vmem(2, 2 * ROWS, BLK),
        vmem(2, 2 * ROWS, BLK),
        vmem(2, BLK, 4 * BLK),
        vmem(SECTIONS, HIDDEN, 2, BLK, BLK),
        vmem(2, 4 * BLK, BLK),
        vmem(SECTIONS, HIDDEN, 2 * ROWS, BLK),
        vmem(SECTIONS, HIDDEN, 2 * ROWS, BLK),
        vmem(SECTIONS + 1, HIDDEN, 2 * ROWS, BLK),
        vmem(HIDDEN, 2 * ROWS, BLK),
        vmem(HIDDEN, ROWS, BLK),
        vmem(HIDDEN, ROWS, BLK, dtype=F32),
        vmem(HIDDEN, ROWS, BLK, dtype=F32),
        vmem(SECTIONS, HIDDEN, ROWS, BLK),
        vmem(SECTIONS, HIDDEN, ROWS, BLK),
    ]
    for count in (16, 8, 4, 2, 2, 1):
        lead = (count,) if count > 1 else ()
        scratch += [vmem(SECTIONS, *lead, *sec), vmem(*lead, *con), vmem(*lead, *exp)]
    scratch += [vmem(2, ROWS, BLK), vmem(2, ROWS, BLK)]
    scratch += [
        pltpu.SemaphoreType.DMA((COPIES,)),
        pltpu.SemaphoreType.DMA((COPIES,)),
        pltpu.SemaphoreType.DMA((COPIES,)),
    ]
    return pl.pallas_call(
        lambda *refs: kernel(scale, *refs),
        out_shape=(
            jax.ShapeDtypeStruct((ROWS, 2 * BLK), BF16),
            jax.ShapeDtypeStruct((ROWS, 2 * BLK), BF16),
            jax.ShapeDtypeStruct((2, 16, 4 * BLK), BF16),
            jax.ShapeDtypeStruct((SECTIONS, HIDDEN, 2, 16, BLK), BF16),
            jax.ShapeDtypeStruct((2, 64, BLK), BF16),
        ),
        in_specs=[pl.BlockSpec(memory_space=pltpu.SMEM)] + [hbm] * 5,
        out_specs=(hbm,) * 5,
        scratch_shapes=scratch,
        compiler_params=pltpu.CompilerParams(
            collective_id=0, has_side_effects=True, vmem_limit_bytes=58 * 2**20
        ),
        name="butterfly",
    )(pattern, tokens, expand_weight, section_weight, contract_weight, cotangent)


def solution(mesh):
    return jax.shard_map(
        body,
        mesh=mesh,
        in_specs=(
            P("dp", "mp"),
            P("mp", None, None),
            P(None, "mp", None, None, None),
            P("mp", None, None),
            P(),
            P("dp", "mp"),
        ),
        out_specs=(
            P("dp", "mp"),
            P("dp", "mp"),
            P("mp", "dp", None),
            P(None, "mp", None, "dp", None),
            P("mp", "dp", None),
        ),
        check_vma=False,
    )
```

```python
import math

import jax
import jax.numpy as jnp
from jax import lax
from jax.experimental import pallas as pl
from jax.experimental.pallas import tpu as pltpu
from jax.sharding import PartitionSpec as P

MESH = pl.DeviceIdType.MESH
BF16, F32 = jnp.bfloat16, jnp.float32
BLK = 256
ROWS = 128
CHUNKS = 2
PIECE = ROWS // CHUNKS
SECTIONS = 4
HIDDEN = 8
HALF = 4
SHARDS = 16
COPIES = 96
SHIFTS = 6


def dot(left, right, left_dim, right_dim):
    return lax.dot_general(
        left, right, (((left_dim,), (right_dim,)), ((), ())), preferred_element_type=F32
    )


def each(count, unroll, step):
    def several(at, carry):
        for more in range(unroll):
            step(at * unroll + more)
        return carry

    lax.fori_loop(0, count // unroll, several, 0)


def kernel(
    scale, pattern, tokens_hbm, expand_hbm, section_hbm, contract_hbm, cot_hbm,
    out_hbm, in_grad_hbm, expand_grad_hbm, section_grad_hbm, contract_grad_hbm,
    tok, cot, expand_w, section_w, contract_w, chosen, paired, grads, act, hidden, total, gelu_grad,
    u_out, u_in, part_s, part_c, part_e, r1_s, r1_c, r1_e, r2_s, r2_c, r2_e, r3_s, r3_c, r3_e,
    fin_s, fin_c, fin_e, far_s, far_c, far_e, out_v, in_grad_v, out_back, in_grad_back,
    send_sem, recv_sem, local_sem, shift_send, shift_recv, shift_local,
):
    dp, mp = lax.axis_index("dp"), lax.axis_index("mp")
    core = mp % 2
    zh, y = dp // 4, dp % 4
    near_y, cross_y = y + 1 - 2 * (y % 2), 3 - y
    near_z, cross_z = zh + 1 - 2 * (zh % 2), 3 - zh
    ya = near_y + core * (cross_y - near_y)
    yb = cross_y + core * (near_y - cross_y)
    za = near_z + core * (cross_z - near_z)
    zb = cross_z + core * (near_z - cross_z)
    to_ya, to_yb = (zh * 4 + ya, mp), (zh * 4 + yb, mp)
    to_za, to_zb = (za * 4 + y, mp), (zb * 4 + y, mp)
    across = [
        (dp, mp + 2**k - 2 * 2**k * ((mp // 2**k) % 2)) for k in range(SECTIONS)
    ]
    z_low = (mp // 2) % 2
    before, after = (zh + 3) % 4, (zh + 1) % 4
    to_before, to_after = (before * 4 + y, mp), (after * 4 + y, mp)
    other_way = (
        (before + z_low * (after - before)) * 4 + y,
        mp + 2 - 4 * z_low,
    )
    half = (y + y // 2) % 2 * (1 - core) + y // 2 * core
    mine, theirs = half * HALF, (1 - half) * HALF

    def split(own, other):
        low, high = (own + other) % 2, (own // 2 + other // 2) % 2
        both = (low + high) % 2
        return both + core * (high - both), high + core * (both - high)

    slot = []
    for shard in range(SHARDS):
        z_first, z_second = split(zh, shard // 4)
        y_last, y_first = split(y, shard % 4)
        slot.append(8 * y_first + 4 * z_first + 2 * z_second + y_last)

    loads, sends = [], []

    def load(src, dst):
        copy = pltpu.make_async_copy(src, dst, local_sem.at[len(loads)])
        copy.start()
        loads.append(copy)
        return copy

    def send(src, dst, device):
        at = len(sends)
        copy = pltpu.make_async_remote_copy(
            src_ref=src,
            dst_ref=dst,
            send_sem=send_sem.at[at],
            recv_sem=recv_sem.at[at],
            device_id=device,
            device_id_type=MESH,
        )
        copy.start()
        sends.append(copy)
        return copy

    class Shift:
        def __init__(self, at, src, dst, device):
            self.near = pltpu.make_async_copy(src, dst, shift_local.at[at])
            self.far = pltpu.make_async_remote_copy(
                src_ref=src,
                dst_ref=dst,
                send_sem=shift_send.at[at],
                recv_sem=shift_recv.at[at],
                device_id=device,
                device_id_type=MESH,
            )

            @pl.when(z_low == 0)
            def _():
                self.near.start()

            @pl.when(z_low == 1)
            def _():
                self.far.start()

        def wait(self):
            @pl.when(z_low == 0)
            def _():
                self.near.wait()

            @pl.when(z_low == 1)
            def _():
                self.far.wait_recv()

        def sent(self):
            @pl.when(z_low == 1)
            def _():
                self.far.wait_send()

    tok_in = [load(tokens_hbm.at[pl.ds(0, PIECE), pl.ds(j * BLK, BLK)], tok.at[j, pl.ds(0, PIECE)]) for j in range(2)]
    expand_in = load(expand_hbm, expand_w)
    section_in = [load(section_hbm.at[0], section_w.at[0])]
    cot_in = [load(cot_hbm.at[pl.ds(0, PIECE), pl.ds(j * BLK, BLK)], cot.at[j, pl.ds(0, PIECE)]) for j in range(2)]
    contract_in = load(contract_hbm, contract_w)
    section_in += [load(section_hbm.at[k], section_w.at[k]) for k in range(1, SECTIONS)]

    barrier = pltpu.get_barrier_semaphore()
    peers = [*across, other_way, to_ya, to_yb, to_za, to_zb]
    for device in peers:
        pl.semaphore_signal(barrier, inc=1, device_id=device, device_id_type=MESH)

    pl.semaphore_wait(barrier, len(peers))
    shifts = [
        Shift(
            2 * at + j,
            src.at[pl.ds(PIECE, PIECE), pl.ds(j * BLK, BLK)],
            dst.at[j, pl.ds(PIECE, PIECE)],
            to_before,
        )
        for at, (src, dst) in enumerate(((tokens_hbm, tok), (cot_hbm, cot)))
        for j in range(2)
    ]

    inverse = []
    for k in range(SECTIONS):
        row = []
        for c in range(HIDDEN):
            place = jnp.int32(0)
            for m in range(1, HIDDEN):
                place = jnp.where(pattern[k, m] == c, jnp.int32(m), place)
            row.append(place)
        inverse.append(row)

    def rows(piece):
        return pl.ds(piece * PIECE, PIECE)

    def expand(piece):
        for j in range(2):
            source = tok[j, rows(piece)]
            for i in range(4):
                hidden[j * 4 + i, rows(piece)] = dot(
                    source, expand_w[j, :, i * BLK : (i + 1) * BLK], 1, 0
                ).astype(BF16)

    def choose(k, piece):
        for m in range(HIDDEN):
            chosen[k, m, rows(piece)] = hidden[pattern[k, m], rows(piece)]

    def partner(k, piece):
        return other_way if k == 1 and piece == 1 else across[k]

    def exchange(k, piece):
        return send(
            chosen.at[k, :, rows(piece)],
            paired.at[k, :, rows(piece)],
            partner(k, piece),
        )

    def own_part(k, piece):
        def one(b):
            total[b, rows(piece)] = dot(
                chosen[k, b, rows(piece)], section_w[k, b, 0], 1, 0
            )

        each(HIDDEN, 4, one)

    def pair_part(k, piece, use):
        def one(b):
            use(
                b,
                total[b, rows(piece)]
                + dot(paired[k, b, rows(piece)], section_w[k, b, 1], 1, 0),
            )

        each(HIDDEN, 4, one)

    def to_hidden(piece):
        def use(b, value):
            hidden[b, rows(piece)] = value.astype(BF16)

        return use

    def to_gelu(piece):
        def use(b, z):
            below = 0.5 * (1.0 + lax.erf(z * math.sqrt(0.5)))
            act[b, rows(piece)] = (z * below).astype(BF16)
            slope = below + z * (jnp.exp(-0.5 * z * z) * (1.0 / math.sqrt(2.0 * math.pi)))
            grads[SECTIONS, b, rows(piece)] = (
                gelu_grad[b, rows(piece)] * slope
            ).astype(BF16)

        return use

    def share(ref, first=0, count=ROWS):
        part = ref.at[pl.ds(theirs, HALF)]
        return send(
            part.at[:, pl.ds(first, count)], part.at[:, pl.ds(ROWS + first, count)], to_ya
        )

    def share_piece(name, ref, piece):
        shared.setdefault(name, []).append(share(ref, piece * PIECE, PIECE))

    def share_feature(ref):
        part = ref.at[1 - half]
        return send(part.at[pl.ds(0, ROWS)], part.at[pl.ds(ROWS, ROWS)], to_ya)

    def back(k, piece):
        def far(b):
            u_out[k, b, rows(piece)] = dot(
                grads[k + 1, b, rows(piece)], section_w[k, b, 1], 1, 1
            ).astype(BF16)

        each(HIDDEN, 4, far)
        copy = send(u_out.at[k, :, rows(piece)], u_in.at[k, :, rows(piece)], partner(k, piece))

        def near(b):
            total[b, rows(piece)] = dot(
                grads[k + 1, b, rows(piece)], section_w[k, b, 0], 1, 1
            )

        each(HIDDEN, 4, near)
        return copy

    def gather_back(k, piece):
        def one(b):
            hidden[b, rows(piece)] = (
                total[b, rows(piece)] + u_in[k, b, rows(piece)].astype(F32)
            ).astype(BF16)

        each(HIDDEN, 4, one)
        for c in range(HIDDEN):
            grads[k, c, rows(piece)] = hidden[inverse[k][c], rows(piece)]

    class Reduction:
        def __init__(self, part, r1, r2, r3, fin, far, unroll):
            self.part, self.r1, self.r2, self.r3 = part, r1, r2, r3
            self.fin, self.far, self.unroll = fin, far, unroll

        def first(self):
            self.copy = send(self.part.at[pl.ds(8, 8)], self.r1, to_yb)

        def add(self, received, count):
            def one(at):
                self.part[at] = (
                    self.part[at].astype(F32) + received[at].astype(F32)
                ).astype(BF16)

            each(count, self.unroll, one)

        def second(self):
            self.copy.wait_recv()
            self.add(self.r1, 8)
            self.copy = send(self.part.at[pl.ds(4, 4)], self.r2, to_za)

        def third(self):
            self.copy.wait_recv()
            self.add(self.r2, 4)
            self.copy = send(self.part.at[pl.ds(2, 2)], self.r3, to_zb)

        def fourth(self, own):
            self.copy.wait_recv()
            for at in range(2):
                self.fin[at] = (
                    (self.part[at].astype(F32) + self.r3[at].astype(F32)) * scale
                ).astype(BF16)
            self.copy = send(self.fin.at[1], self.far, to_ya)
            load(self.fin.at[0], own)

        def fifth(self, other):
            self.copy.wait_recv()
            load(self.far, other)

    reduce_s = [
        Reduction(part_s.at[k], r1_s.at[k], r2_s.at[k], r3_s.at[k], fin_s.at[k], far_s.at[k], 1)
        for k in range(SECTIONS)
    ]
    reduce_c = Reduction(part_c, r1_c, r2_c, r3_c, fin_c, far_c, 2)
    reduce_e = Reduction(part_e, r1_e, r2_e, r3_e, fin_e, far_e, 2)

    def section_terms(k):
        for i in range(HALF):
            upstream = grads[k + 1, mine + i]
            for s, ref in enumerate((chosen, paired)):
                term = dot(ref[k, mine + i], upstream, 0, 0).astype(BF16)
                for shard in range(SHARDS):
                    part_s[k, slot[shard], i, s] = term[shard * 16 : (shard + 1) * 16]
        reduce_s[k].first()

    def contract_terms():
        for i in range(HALF):
            term = dot(act[mine + i], cot[half], 0, 0).astype(BF16)
            for q in range(4):
                part_c[slot[i * 4 + q]] = term[q * 64 : (q + 1) * 64]
        reduce_c.first()

    def expand_terms():
        for i in range(HALF):
            term = dot(tok[half], grads[0, mine + i], 0, 0).astype(BF16)
            for shard in range(SHARDS):
                part_e[slot[shard], :, i * BLK : (i + 1) * BLK] = term[shard * 16 : (shard + 1) * 16]
        reduce_e.first()

    pieces = range(CHUNKS)
    coming = [None] * CHUNKS
    shared = {}

    for copy in tok_in:
        copy.wait()
    expand_in.wait()
    for piece in pieces:
        if piece == 1:
            for shift in shifts[:2]:
                shift.wait()
        expand(piece)
        choose(0, piece)
        coming[piece] = exchange(0, piece)
        if piece == 0:
            section_in[0].wait()
        own_part(0, piece)
    shared["tok"] = share_feature(tok)
    shared["own", 0] = share(chosen.at[0])
    for k in range(SECTIONS - 1):
        section_in[k + 1].wait()
        for piece in pieces:
            coming[piece].wait_recv()
            pair_part(k, piece, to_hidden(piece))
            choose(k + 1, piece)
            coming[piece] = exchange(k + 1, piece)
            own_part(k + 1, piece)
        shared["pair", k] = share(paired.at[k])
        shared["own", k + 1] = share(chosen.at[k + 1])
        if k == 0:
            for copy in [*cot_in, *shifts[2:]]:
                copy.wait()
            contract_in.wait()
            shared["cot"] = share_feature(cot)

            def gelu_grads(j):
                source = cot[j, pl.ds(0, ROWS)]
                for i in range(4):
                    gelu_grad[j * 4 + i] = dot(
                        source, contract_w[j, i * BLK : (i + 1) * BLK], 1, 1
                    )

            each(2, 1, gelu_grads)

    for piece in pieces:
        coming[piece].wait_recv()
        share_piece(("pair", SECTIONS - 1), paired.at[SECTIONS - 1], piece)
        pair_part(SECTIONS - 1, piece, to_gelu(piece))
        coming[piece] = back(SECTIONS - 1, piece)
        share_piece("act", act, piece)
        share_piece(("grad", SECTIONS), grads.at[SECTIONS], piece)

    def outputs(j):
        sums = sum(
            dot(act[j * 4 + i, pl.ds(0, ROWS)], contract_w[j, i * BLK : (i + 1) * BLK], 1, 0)
            for i in range(4)
        )
        out_v[j] = sums.astype(BF16)

    each(2, 1, outputs)

    def hand_back(at, ref, back_ref, result):
        for j in range(2):
            load(ref.at[j, rows(0)], result.at[rows(0), pl.ds(j * BLK, BLK)])
        return Shift(at, ref.at[:, rows(1)], back_ref, to_after)

    def take_back(shift, back_ref, result):
        shift.wait()
        for j in range(2):
            load(back_ref.at[j], result.at[rows(1), pl.ds(j * BLK, BLK)])

    shifts.append(hand_back(4, out_v, out_back, out_hbm))

    def await_shared(*names):
        for name in names:
            copies = shared[name]
            for copy in copies if isinstance(copies, list) else [copies]:
                copy.wait_recv()

    def section_first(k):
        await_shared(("grad", k + 1), ("own", k), ("pair", k))
        section_terms(k)

    def step(k, piece):
        coming[piece].wait_recv()
        gather_back(k, piece)
        if k:
            coming[piece] = back(k - 1, piece)
        share_piece(("grad", k), grads.at[k], piece)

    def own_grad(k):
        return section_grad_hbm.at[k, pl.ds(mine, HALF)]

    def far_grad(k):
        return section_grad_hbm.at[k, pl.ds(theirs, HALF)]

    step(3, 0)
    await_shared("act", "cot")
    contract_terms()
    section_first(3)
    step(3, 1)
    reduce_c.second()
    step(2, 0)
    section_first(2)
    step(2, 1)
    reduce_s[3].second()
    reduce_c.third()
    step(1, 0)
    section_first(1)
    step(1, 1)
    step(0, 0)
    step(0, 1)
    reduce_s[2].second()
    reduce_s[3].third()
    reduce_c.fourth(contract_grad_hbm.at[half])
    section_first(0)
    reduce_s[1].second()
    await_shared("tok", ("grad", 0))
    expand_terms()
    reduce_s[2].third()
    reduce_s[3].fourth(own_grad(3))
    reduce_s[0].second()
    reduce_e.second()
    take_back(shifts[4], out_back, out_hbm)
    for j in range(2):
        sums = sum(
            dot(grads[0, j * 4 + i, pl.ds(0, ROWS)], expand_w[j, :, i * BLK : (i + 1) * BLK], 1, 1)
            for i in range(4)
        )
        in_grad_v[j] = sums.astype(BF16)
    shifts.append(hand_back(5, in_grad_v, in_grad_back, in_grad_hbm))
    reduce_s[1].third()
    reduce_c.fifth(contract_grad_hbm.at[1 - half])
    reduce_s[2].fourth(own_grad(2))
    reduce_s[0].third()
    reduce_e.third()
    reduce_s[1].fourth(own_grad(1))
    reduce_s[3].fifth(far_grad(3))
    take_back(shifts[5], in_grad_back, in_grad_hbm)
    reduce_s[0].fourth(own_grad(0))
    reduce_s[2].fifth(far_grad(2))
    reduce_e.fourth(expand_grad_hbm.at[half])
    reduce_s[1].fifth(far_grad(1))
    reduce_s[0].fifth(far_grad(0))
    reduce_e.fifth(expand_grad_hbm.at[1 - half])
    for shift in shifts:
        shift.sent()
    for copy in sends:
        copy.wait_send()
    for copy in loads[len(tok_in) + len(cot_in) + 2 + SECTIONS :]:
        copy.wait()


def hand_over(*refs):
    count = len(refs) // 2
    for at in range(count):
        refs[count + at][...] = refs[at][...]


def body(tokens, expand_weight, section_weight, contract_weight, pattern, cotangent):
    scale = 1.0 / math.sqrt(tokens.shape[0] * lax.axis_size("dp"))
    hbm = pl.BlockSpec(memory_space=pl.ANY)

    def vmem(*shape, dtype=BF16):
        return pltpu.VMEM(shape, dtype)

    sec, con, exp = (HALF, 2, 16, BLK), (64, BLK), (16, 4 * BLK)
    scratch = [
        vmem(2, 2 * ROWS, BLK),
        vmem(2, 2 * ROWS, BLK),
        vmem(2, BLK, 4 * BLK),
        vmem(SECTIONS, HIDDEN, 2, BLK, BLK),
        vmem(2, 4 * BLK, BLK),
        vmem(SECTIONS, HIDDEN, 2 * ROWS, BLK),
        vmem(SECTIONS, HIDDEN, 2 * ROWS, BLK),
        vmem(SECTIONS + 1, HIDDEN, 2 * ROWS, BLK),
        vmem(HIDDEN, 2 * ROWS, BLK),
        vmem(HIDDEN, ROWS, BLK),
        vmem(HIDDEN, ROWS, BLK, dtype=F32),
        vmem(HIDDEN, ROWS, BLK, dtype=F32),
        vmem(SECTIONS, HIDDEN, ROWS, BLK),
        vmem(SECTIONS, HIDDEN, ROWS, BLK),
    ]
    for count in (16, 8, 4, 2, 2, 1):
        lead = (count,) if count > 1 else ()
        scratch += [vmem(SECTIONS, *lead, *sec), vmem(*lead, *con), vmem(*lead, *exp)]
    scratch += [vmem(2, ROWS, BLK), vmem(2, ROWS, BLK)]
    scratch += [vmem(2, PIECE, BLK), vmem(2, PIECE, BLK)]
    scratch += [
        pltpu.SemaphoreType.DMA((COPIES,)),
        pltpu.SemaphoreType.DMA((COPIES,)),
        pltpu.SemaphoreType.DMA((COPIES,)),
        pltpu.SemaphoreType.DMA((SHIFTS,)),
        pltpu.SemaphoreType.DMA((SHIFTS,)),
        pltpu.SemaphoreType.DMA((SHIFTS,)),
    ]
    shapes = (
        jax.ShapeDtypeStruct((ROWS, 2 * BLK), BF16),
        jax.ShapeDtypeStruct((ROWS, 2 * BLK), BF16),
        jax.ShapeDtypeStruct((2, 16, 4 * BLK), BF16),
        jax.ShapeDtypeStruct((SECTIONS, HIDDEN, 2, 16, BLK), BF16),
        jax.ShapeDtypeStruct((2, 64, BLK), BF16),
    )
    results = pl.pallas_call(
        lambda *refs: kernel(scale, *refs),
        out_shape=shapes,
        in_specs=[pl.BlockSpec(memory_space=pltpu.SMEM)] + [hbm] * 5,
        out_specs=(hbm,) * 5,
        scratch_shapes=scratch,
        compiler_params=pltpu.CompilerParams(
            collective_id=0, has_side_effects=True, vmem_limit_bytes=58 * 2**20
        ),
        name="butterfly",
    )(pattern, tokens, expand_weight, section_weight, contract_weight, cotangent)
    whole = pl.BlockSpec(memory_space=pltpu.VMEM)
    return pl.pallas_call(
        hand_over,
        out_shape=shapes,
        in_specs=[whole] * 5,
        out_specs=(whole,) * 5,
        name="hand_over",
    )(*results)


def solution(mesh):
    return jax.shard_map(
        body,
        mesh=mesh,
        in_specs=(
            P("dp", "mp"),
            P("mp", None, None),
            P(None, "mp", None, None, None),
            P("mp", None, None),
            P(),
            P("dp", "mp"),
        ),
        out_specs=(
            P("dp", "mp"),
            P("dp", "mp"),
            P("mp", "dp", None),
            P(None, "mp", None, "dp", None),
            P("mp", "dp", None),
        ),
        check_vma=False,
    )
```

```python
import math

import jax
import jax.numpy as jnp
from jax import lax
from jax.experimental import pallas as pl
from jax.experimental.pallas import tpu as pltpu
from jax.sharding import PartitionSpec as P

MESH = pl.DeviceIdType.MESH
BF16, F32 = jnp.bfloat16, jnp.float32
BLK = 256
ROWS = 128
CHUNKS = 2
PIECE = ROWS // CHUNKS
SECTIONS = 4
HIDDEN = 8
HALF = 4
SHARDS = 16
COPIES = 96
SHIFTS = 6


def dot(left, right, left_dim, right_dim):
    return lax.dot_general(
        left, right, (((left_dim,), (right_dim,)), ((), ())), preferred_element_type=F32
    )


def each(count, unroll, step):
    def several(at, carry):
        for more in range(unroll):
            step(at * unroll + more)
        return carry

    lax.fori_loop(0, count // unroll, several, 0)


def kernel(
    scale, pattern, tokens_hbm, expand_hbm, section_hbm, contract_hbm, cot_hbm,
    out_hbm, in_grad_hbm, expand_grad_hbm, section_grad_hbm, contract_grad_hbm,
    tok, cot, expand_w, section_w, contract_w, chosen, paired, grads, act, hidden, total, gelu_grad,
    u_out, u_in, part_s, part_c, part_e, r1_s, r1_c, r1_e, r2_s, r2_c, r2_e, r3_s, r3_c, r3_e,
    fin_s, fin_c, fin_e, far_s, far_c, far_e, out_v, in_grad_v, out_back, in_grad_back,
    send_sem, recv_sem, local_sem, shift_send, shift_recv, shift_local,
):
    dp, mp = lax.axis_index("dp"), lax.axis_index("mp")
    core = mp % 2
    zh, y = dp // 4, dp % 4
    near_y, cross_y = y + 1 - 2 * (y % 2), 3 - y
    near_z, cross_z = zh + 1 - 2 * (zh % 2), 3 - zh
    ya = near_y + core * (cross_y - near_y)
    yb = cross_y + core * (near_y - cross_y)
    za = near_z + core * (cross_z - near_z)
    zb = cross_z + core * (near_z - cross_z)
    to_ya, to_yb = (zh * 4 + ya, mp), (zh * 4 + yb, mp)
    to_za, to_zb = (za * 4 + y, mp), (zb * 4 + y, mp)
    across = [
        (dp, mp + 2**k - 2 * 2**k * ((mp // 2**k) % 2)) for k in range(SECTIONS)
    ]
    z_low = (mp // 2) % 2
    before, after = (zh + 3) % 4, (zh + 1) % 4
    to_before, to_after = (before * 4 + y, mp), (after * 4 + y, mp)
    other_way = (
        (before + z_low * (after - before)) * 4 + y,
        mp + 2 - 4 * z_low,
    )
    half = (y + y // 2) % 2 * (1 - core) + y // 2 * core
    mine, theirs = half * HALF, (1 - half) * HALF

    def split(own, other):
        low, high = (own + other) % 2, (own // 2 + other // 2) % 2
        both = (low + high) % 2
        return both + core * (high - both), high + core * (both - high)

    slot = []
    for shard in range(SHARDS):
        z_first, z_second = split(zh, shard // 4)
        y_last, y_first = split(y, shard % 4)
        slot.append(8 * y_first + 4 * z_first + 2 * z_second + y_last)

    loads, sends = [], []

    def load(src, dst):
        copy = pltpu.make_async_copy(src, dst, local_sem.at[len(loads)])
        copy.start()
        loads.append(copy)
        return copy

    def send(src, dst, device):
        at = len(sends)
        copy = pltpu.make_async_remote_copy(
            src_ref=src,
            dst_ref=dst,
            send_sem=send_sem.at[at],
            recv_sem=recv_sem.at[at],
            device_id=device,
            device_id_type=MESH,
        )
        copy.start()
        sends.append(copy)
        return copy

    class Shift:
        def __init__(self, at, src, dst, device):
            self.near = pltpu.make_async_copy(src, dst, shift_local.at[at])
            self.far = pltpu.make_async_remote_copy(
                src_ref=src,
                dst_ref=dst,
                send_sem=shift_send.at[at],
                recv_sem=shift_recv.at[at],
                device_id=device,
                device_id_type=MESH,
            )

            @pl.when(z_low == 0)
            def _():
                self.near.start()

            @pl.when(z_low == 1)
            def _():
                self.far.start()

        def wait(self):
            @pl.when(z_low == 0)
            def _():
                self.near.wait()

            @pl.when(z_low == 1)
            def _():
                self.far.wait_recv()

        def sent(self):
            @pl.when(z_low == 1)
            def _():
                self.far.wait_send()

    tok_in = [load(tokens_hbm.at[pl.ds(0, PIECE), pl.ds(j * BLK, BLK)], tok.at[j, pl.ds(0, PIECE)]) for j in range(2)]
    expand_in = load(expand_hbm, expand_w)
    section_in = [load(section_hbm.at[0], section_w.at[0])]
    cot_in = [load(cot_hbm.at[pl.ds(0, PIECE), pl.ds(j * BLK, BLK)], cot.at[j, pl.ds(0, PIECE)]) for j in range(2)]
    contract_in = load(contract_hbm, contract_w)
    section_in += [load(section_hbm.at[k], section_w.at[k]) for k in range(1, SECTIONS)]

    barrier = pltpu.get_barrier_semaphore()
    peers = [*across, other_way, to_ya, to_yb, to_za, to_zb]
    for device in peers:
        pl.semaphore_signal(barrier, inc=1, device_id=device, device_id_type=MESH)

    pl.semaphore_wait(barrier, len(peers))
    shifts = [
        Shift(
            2 * at + j,
            src.at[pl.ds(PIECE, PIECE), pl.ds(j * BLK, BLK)],
            dst.at[j, pl.ds(PIECE, PIECE)],
            to_before,
        )
        for at, (src, dst) in enumerate(((tokens_hbm, tok), (cot_hbm, cot)))
        for j in range(2)
    ]

    inverse = []
    for k in range(SECTIONS):
        row = []
        for c in range(HIDDEN):
            place = jnp.int32(0)
            for m in range(1, HIDDEN):
                place = jnp.where(pattern[k, m] == c, jnp.int32(m), place)
            row.append(place)
        inverse.append(row)

    def rows(piece):
        return pl.ds(piece * PIECE, PIECE)

    def expand(piece):
        for j in range(2):
            source = tok[j, rows(piece)]
            for i in range(4):
                hidden[j * 4 + i, rows(piece)] = dot(
                    source, expand_w[j, :, i * BLK : (i + 1) * BLK], 1, 0
                ).astype(BF16)

    def choose(k, piece):
        for m in range(HIDDEN):
            chosen[k, m, rows(piece)] = hidden[pattern[k, m], rows(piece)]

    def partner(k, piece):
        return other_way if k == 1 and piece == 1 else across[k]

    def exchange(k, piece):
        return send(
            chosen.at[k, :, rows(piece)],
            paired.at[k, :, rows(piece)],
            partner(k, piece),
        )

    def own_part(k, piece):
        def one(b):
            total[b, rows(piece)] = dot(
                chosen[k, b, rows(piece)], section_w[k, b, 0], 1, 0
            )

        each(HIDDEN, 4, one)

    def pair_part(k, piece, use):
        def one(b):
            use(
                b,
                total[b, rows(piece)]
                + dot(paired[k, b, rows(piece)], section_w[k, b, 1], 1, 0),
            )

        each(HIDDEN, 4, one)

    def to_hidden(piece):
        def use(b, value):
            hidden[b, rows(piece)] = value.astype(BF16)

        return use

    def to_gelu(piece):
        def use(b, z):
            below = 0.5 * (1.0 + lax.erf(z * math.sqrt(0.5)))
            act[b, rows(piece)] = (z * below).astype(BF16)
            slope = below + z * (jnp.exp(-0.5 * z * z) * (1.0 / math.sqrt(2.0 * math.pi)))
            grads[SECTIONS, b, rows(piece)] = (
                gelu_grad[b, rows(piece)] * slope
            ).astype(BF16)

        return use

    def share(ref, first=0, count=ROWS):
        part = ref.at[pl.ds(theirs, HALF)]
        return send(
            part.at[:, pl.ds(first, count)], part.at[:, pl.ds(ROWS + first, count)], to_ya
        )

    def share_piece(name, ref, piece):
        shared.setdefault(name, []).append(share(ref, piece * PIECE, PIECE))

    def share_feature(ref):
        part = ref.at[1 - half]
        return send(part.at[pl.ds(0, ROWS)], part.at[pl.ds(ROWS, ROWS)], to_ya)

    def back(k, piece):
        def far(b):
            u_out[k, b, rows(piece)] = dot(
                grads[k + 1, b, rows(piece)], section_w[k, b, 1], 1, 1
            ).astype(BF16)

        each(HIDDEN, 4, far)
        copy = send(u_out.at[k, :, rows(piece)], u_in.at[k, :, rows(piece)], partner(k, piece))

        def near(b):
            total[b, rows(piece)] = dot(
                grads[k + 1, b, rows(piece)], section_w[k, b, 0], 1, 1
            )

        each(HIDDEN, 4, near)
        return copy

    def gather_back(k, piece):
        def one(b):
            hidden[b, rows(piece)] = (
                total[b, rows(piece)] + u_in[k, b, rows(piece)].astype(F32)
            ).astype(BF16)

        each(HIDDEN, 4, one)
        for c in range(HIDDEN):
            grads[k, c, rows(piece)] = hidden[inverse[k][c], rows(piece)]

    class Reduction:
        def __init__(self, part, r1, r2, r3, fin, far, unroll):
            self.part, self.r1, self.r2, self.r3 = part, r1, r2, r3
            self.fin, self.far, self.unroll = fin, far, unroll

        def first(self):
            self.copy = send(self.part.at[pl.ds(8, 8)], self.r1, to_yb)

        def add(self, received, count):
            def one(at):
                self.part[at] = (
                    self.part[at].astype(F32) + received[at].astype(F32)
                ).astype(BF16)

            each(count, self.unroll, one)

        def second(self):
            self.copy.wait_recv()
            self.add(self.r1, 8)
            self.copy = send(self.part.at[pl.ds(4, 4)], self.r2, to_za)

        def third(self):
            self.copy.wait_recv()
            self.add(self.r2, 4)
            self.copy = send(self.part.at[pl.ds(2, 2)], self.r3, to_zb)

        def fourth(self, own):
            self.copy.wait_recv()
            for at in range(2):
                self.fin[at] = (
                    (self.part[at].astype(F32) + self.r3[at].astype(F32)) * scale
                ).astype(BF16)
            self.copy = send(self.fin.at[1], self.far, to_ya)
            load(self.fin.at[0], own)

        def fifth(self, other):
            self.copy.wait_recv()
            load(self.far, other)

    class Sections:
        def __init__(self, k):
            self.k, self.halves = k, []
            for h in range(2):
                part = pl.ds(2 * h, 2)
                self.halves.append(
                    Reduction(
                        *(ref.at[k, :, part] for ref in (part_s, r1_s, r2_s, r3_s, fin_s)),
                        far_s.at[k, part],
                        2,
                    )
                )

        def second(self):
            for one in self.halves:
                one.second()

        def third(self):
            for one in self.halves:
                one.third()

        def fourth(self):
            for h, one in enumerate(self.halves):
                one.fourth(section_grad_hbm.at[self.k, pl.ds(mine + 2 * h, 2)])

        def fifth(self):
            for h, one in enumerate(self.halves):
                one.fifth(section_grad_hbm.at[self.k, pl.ds(theirs + 2 * h, 2)])

    reduce_s = [Sections(k) for k in range(SECTIONS)]
    reduce_c = Reduction(part_c, r1_c, r2_c, r3_c, fin_c, far_c, 2)
    reduce_e = Reduction(part_e, r1_e, r2_e, r3_e, fin_e, far_e, 2)

    def section_terms(k):
        for i in range(HALF):
            upstream = grads[k + 1, mine + i]
            for s, ref in enumerate((chosen, paired)):
                term = dot(ref[k, mine + i], upstream, 0, 0).astype(BF16)
                for shard in range(SHARDS):
                    part_s[k, slot[shard], i, s] = term[shard * 16 : (shard + 1) * 16]
            if i % 2:
                reduce_s[k].halves[i // 2].first()

    def contract_terms():
        for i in range(HALF):
            term = dot(act[mine + i], cot[half], 0, 0).astype(BF16)
            for q in range(4):
                part_c[slot[i * 4 + q]] = term[q * 64 : (q + 1) * 64]
        reduce_c.first()

    def expand_terms():
        for i in range(HALF):
            term = dot(tok[half], grads[0, mine + i], 0, 0).astype(BF16)
            for shard in range(SHARDS):
                part_e[slot[shard], :, i * BLK : (i + 1) * BLK] = term[shard * 16 : (shard + 1) * 16]
        reduce_e.first()

    pieces = range(CHUNKS)
    coming = [None] * CHUNKS
    shared = {}

    for copy in tok_in:
        copy.wait()
    expand_in.wait()
    for piece in pieces:
        if piece == 1:
            for shift in shifts[:2]:
                shift.wait()
        expand(piece)
        choose(0, piece)
        coming[piece] = exchange(0, piece)
        if piece == 0:
            section_in[0].wait()
        own_part(0, piece)
    shared["tok"] = share_feature(tok)
    shared["own", 0] = share(chosen.at[0])
    for k in range(SECTIONS - 1):
        section_in[k + 1].wait()
        for piece in pieces:
            coming[piece].wait_recv()
            pair_part(k, piece, to_hidden(piece))
            choose(k + 1, piece)
            coming[piece] = exchange(k + 1, piece)
            own_part(k + 1, piece)
        shared["pair", k] = share(paired.at[k])
        shared["own", k + 1] = share(chosen.at[k + 1])
        if k == 0:
            for copy in [*cot_in, *shifts[2:]]:
                copy.wait()
            contract_in.wait()
            shared["cot"] = share_feature(cot)

            def gelu_grads(j):
                source = cot[j, pl.ds(0, ROWS)]
                for i in range(4):
                    gelu_grad[j * 4 + i] = dot(
                        source, contract_w[j, i * BLK : (i + 1) * BLK], 1, 1
                    )

            each(2, 1, gelu_grads)

    for piece in pieces:
        coming[piece].wait_recv()
        share_piece(("pair", SECTIONS - 1), paired.at[SECTIONS - 1], piece)
        pair_part(SECTIONS - 1, piece, to_gelu(piece))
        coming[piece] = back(SECTIONS - 1, piece)
        share_piece("act", act, piece)
        share_piece(("grad", SECTIONS), grads.at[SECTIONS], piece)

    def outputs(j):
        sums = sum(
            dot(act[j * 4 + i, pl.ds(0, ROWS)], contract_w[j, i * BLK : (i + 1) * BLK], 1, 0)
            for i in range(4)
        )
        out_v[j] = sums.astype(BF16)

    each(2, 1, outputs)

    def hand_back(at, ref, back_ref, result):
        for j in range(2):
            load(ref.at[j, rows(0)], result.at[rows(0), pl.ds(j * BLK, BLK)])
        return Shift(at, ref.at[:, rows(1)], back_ref, to_after)

    def take_back(shift, back_ref, result):
        shift.wait()
        for j in range(2):
            load(back_ref.at[j], result.at[rows(1), pl.ds(j * BLK, BLK)])

    shifts.append(hand_back(4, out_v, out_back, out_hbm))

    def await_shared(*names):
        for name in names:
            copies = shared[name]
            for copy in copies if isinstance(copies, list) else [copies]:
                copy.wait_recv()

    def section_first(k):
        await_shared(("grad", k + 1), ("own", k), ("pair", k))
        section_terms(k)

    def step(k, piece):
        coming[piece].wait_recv()
        gather_back(k, piece)
        if k:
            coming[piece] = back(k - 1, piece)
        share_piece(("grad", k), grads.at[k], piece)

    step(3, 0)
    await_shared("act", "cot")
    contract_terms()
    section_first(3)
    step(3, 1)
    reduce_c.second()
    step(2, 0)
    section_first(2)
    step(2, 1)
    reduce_s[3].second()
    reduce_c.third()
    step(1, 0)
    section_first(1)
    step(1, 1)
    step(0, 0)
    step(0, 1)
    reduce_s[2].second()
    reduce_s[3].third()
    reduce_c.fourth(contract_grad_hbm.at[half])
    section_first(0)
    reduce_s[1].second()
    await_shared("tok", ("grad", 0))
    expand_terms()
    reduce_s[2].third()
    reduce_s[3].fourth()
    reduce_s[0].second()
    reduce_e.second()
    take_back(shifts[4], out_back, out_hbm)
    for j in range(2):
        sums = sum(
            dot(grads[0, j * 4 + i, pl.ds(0, ROWS)], expand_w[j, :, i * BLK : (i + 1) * BLK], 1, 1)
            for i in range(4)
        )
        in_grad_v[j] = sums.astype(BF16)
    shifts.append(hand_back(5, in_grad_v, in_grad_back, in_grad_hbm))
    reduce_s[1].third()
    reduce_c.fifth(contract_grad_hbm.at[1 - half])
    reduce_s[2].fourth()
    reduce_s[0].third()
    reduce_e.third()
    reduce_s[1].fourth()
    reduce_s[3].fifth()
    take_back(shifts[5], in_grad_back, in_grad_hbm)
    reduce_s[0].fourth()
    reduce_s[2].fifth()
    reduce_e.fourth(expand_grad_hbm.at[half])
    reduce_s[1].fifth()
    reduce_s[0].fifth()
    reduce_e.fifth(expand_grad_hbm.at[1 - half])
    for shift in shifts:
        shift.sent()
    for copy in sends:
        copy.wait_send()
    for copy in loads[len(tok_in) + len(cot_in) + 2 + SECTIONS :]:
        copy.wait()


def hand_over(*refs):
    count = len(refs) // 2
    for at in range(count):
        refs[count + at][...] = refs[at][...]


def body(tokens, expand_weight, section_weight, contract_weight, pattern, cotangent):
    scale = 1.0 / math.sqrt(tokens.shape[0] * lax.axis_size("dp"))
    hbm = pl.BlockSpec(memory_space=pl.ANY)

    def vmem(*shape, dtype=BF16):
        return pltpu.VMEM(shape, dtype)

    sec, con, exp = (HALF, 2, 16, BLK), (64, BLK), (16, 4 * BLK)
    scratch = [
        vmem(2, 2 * ROWS, BLK),
        vmem(2, 2 * ROWS, BLK),
        vmem(2, BLK, 4 * BLK),
        vmem(SECTIONS, HIDDEN, 2, BLK, BLK),
        vmem(2, 4 * BLK, BLK),
        vmem(SECTIONS, HIDDEN, 2 * ROWS, BLK),
        vmem(SECTIONS, HIDDEN, 2 * ROWS, BLK),
        vmem(SECTIONS + 1, HIDDEN, 2 * ROWS, BLK),
        vmem(HIDDEN, 2 * ROWS, BLK),
        vmem(HIDDEN, ROWS, BLK),
        vmem(HIDDEN, ROWS, BLK, dtype=F32),
        vmem(HIDDEN, ROWS, BLK, dtype=F32),
        vmem(SECTIONS, HIDDEN, ROWS, BLK),
        vmem(SECTIONS, HIDDEN, ROWS, BLK),
    ]
    for count in (16, 8, 4, 2, 2, 1):
        lead = (count,) if count > 1 else ()
        scratch += [vmem(SECTIONS, *lead, *sec), vmem(*lead, *con), vmem(*lead, *exp)]
    scratch += [vmem(2, ROWS, BLK), vmem(2, ROWS, BLK)]
    scratch += [vmem(2, PIECE, BLK), vmem(2, PIECE, BLK)]
    scratch += [
        pltpu.SemaphoreType.DMA((COPIES,)),
        pltpu.SemaphoreType.DMA((COPIES,)),
        pltpu.SemaphoreType.DMA((COPIES,)),
        pltpu.SemaphoreType.DMA((SHIFTS,)),
        pltpu.SemaphoreType.DMA((SHIFTS,)),
        pltpu.SemaphoreType.DMA((SHIFTS,)),
    ]
    shapes = (
        jax.ShapeDtypeStruct((ROWS, 2 * BLK), BF16),
        jax.ShapeDtypeStruct((ROWS, 2 * BLK), BF16),
        jax.ShapeDtypeStruct((2, 16, 4 * BLK), BF16),
        jax.ShapeDtypeStruct((SECTIONS, HIDDEN, 2, 16, BLK), BF16),
        jax.ShapeDtypeStruct((2, 64, BLK), BF16),
    )
    results = pl.pallas_call(
        lambda *refs: kernel(scale, *refs),
        out_shape=shapes,
        in_specs=[pl.BlockSpec(memory_space=pltpu.SMEM)] + [hbm] * 5,
        out_specs=(hbm,) * 5,
        scratch_shapes=scratch,
        compiler_params=pltpu.CompilerParams(
            collective_id=0, has_side_effects=True, vmem_limit_bytes=58 * 2**20
        ),
        name="butterfly",
    )(pattern, tokens, expand_weight, section_weight, contract_weight, cotangent)
    whole = pl.BlockSpec(memory_space=pltpu.VMEM)
    return pl.pallas_call(
        hand_over,
        out_shape=shapes,
        in_specs=[whole] * 5,
        out_specs=(whole,) * 5,
        name="hand_over",
    )(*results)


def solution(mesh):
    return jax.shard_map(
        body,
        mesh=mesh,
        in_specs=(
            P("dp", "mp"),
            P("mp", None, None),
            P(None, "mp", None, None, None),
            P("mp", None, None),
            P(),
            P("dp", "mp"),
        ),
        out_specs=(
            P("dp", "mp"),
            P("dp", "mp"),
            P("mp", "dp", None),
            P(None, "mp", None, "dp", None),
            P("mp", "dp", None),
        ),
        check_vma=False,
    )
```
